32 devices in a mesh: samp: 4 (over y, x), ind: 8 (over z, core).
Axes of the slice: x: 2, y: 2, z: 4, core: 2. Of those that a mesh axis runs over, the one named last changes fastest.
Arguments:
- points: bfloat16 [8192, 64], P('samp'), may hold values from -6 to 6
- centers: bfloat16 [65536, 64], P('ind'), may hold values from -6 to 6
- coeffs: bfloat16 [65536, 128], P('ind'), may hold values from -0.6 to 0.6
- targets: bfloat16 [8192, 128], P('samp'), may hold values from 0 to 1
- diag_inv: float32 [128, 512, 512], P('ind'), may hold values from -3 to 15
- low_left: bfloat16 [128, 512, 64], P('ind'), may hold values from -0.0014648438 to 0.0014648438
- low_right: bfloat16 [128, 512, 64], P('ind'), may hold values from -0.25 to 0.25
- decay_rates: float32 [128, 64], P('ind'), may hold values from 0.05 to 64
- block_ranks: int32 [128], P('ind'), may hold values from 16 to 64
Outputs:
- direction: float32 [65536, 128], P('ind')
The draws below stay inside these ranges and needn't reach their ends.
All inputs are finite; a program needn't handle non-finite values.
Results may differ from the reference program's by a relative error of at most 0.0003.
Values may be sent and summed in bfloat16 or wider, within the bound.
A program may use at most 128 MiB of HBM per device.

```python
import math
import jax
import jax.numpy as jnp
from jax import lax

D = 64
L = 128
M = 65536
B = 512
R = 64
N = 8192
NB = 128


def draw_coeffs(key, part):
    uniform_key = jax.random.fold_in(key, 0)
    values = jax.random.uniform(uniform_key, (M, L), jnp.float32, -0.3, 0.3)
    return (values - jnp.mean(values, axis=0, keepdims=True)).astype(jnp.bfloat16)


def draw_diag_inv(key, part):
    diag_key, jitter_key = jax.random.split(key)
    leading = jax.random.uniform(diag_key, (NB, B), jnp.float32, 4.0, 12.0)
    jitter = jnp.clip(jax.random.normal(jitter_key, (NB, B, B), jnp.float32), -3.0, 3.0) * (2.0 / math.sqrt(B))
    return jitter + leading[:, :, None] * jnp.eye(B, dtype=jnp.float32)


def with_ends(array, key, low, high):
    shape = array.shape
    place = [jax.random.randint(jax.random.fold_in(key, axis), (), 0, shape[axis]) for axis in range(len(shape))]
    array = array.at[tuple(place)].set(low)
    longest = shape.index(max(shape))
    place[longest] = (place[longest] + 1) % shape[longest]
    return array.at[tuple(place)].set(high)


def block_levels(key, dims, pieces, smallest, top_value):
    level = 1.0
    for dim, shards_of in pieces:
        steps = jax.random.uniform(jax.random.fold_in(jax.random.fold_in(key, 6), dim), (shards_of,), jnp.float32, smallest / len(pieces), top_value / len(pieces))
        level = level * jnp.repeat(jnp.exp(steps), dims[dim] // shards_of).reshape((-1,) + (1,) * (len(dims) - 1 - dim))
    return level


def scatter_about(rng, extent, spread, limit, shards=(), kind=jnp.bfloat16):
    drawn = jax.random.normal(rng, extent, jnp.float32) * spread
    if len(shards) > 0:
        drawn = block_levels(rng, extent, shards, -0.22, 0.18) * drawn
    return jnp.clip(drawn, min=-limit, max=limit).astype(kind)


def setup_inputs(seed: int = 0) -> dict:
    seeds = jax.random.split(jax.random.key(seed), 10)
    return {
        "points": scatter_about(seeds[0], (N, D), 1.0, 6.0, ((0, 4),)),
        "centers": scatter_about(seeds[1], (M, D), 1.0, 6.0, ((0, 8),)),
        "coeffs": draw_coeffs(jax.random.fold_in(seeds[9], 71), 0),
        "targets": jnp.clip(1.0 * jax.random.uniform(seeds[3], (N, L), jnp.float32) ** block_levels(seeds[3], (N, L), ((0, 4),), -0.2, 0.2), 0.0, 1.0).astype(jnp.bfloat16),
        "diag_inv": draw_diag_inv(jax.random.fold_in(seeds[9], 71), 0),
        "low_left": scatter_about(seeds[5], (NB, B, R), (250000 * R) ** -0.5, 0.0014648438, ((0, 8),)),
        "low_right": scatter_about(seeds[6], (NB, B, R), B ** -0.5, 0.25, ((0, 8),)),
        "decay_rates": jnp.clip(jnp.exp(math.log(64.0) - 7.1546153 * jax.random.uniform(seeds[7], (NB, R), jnp.float32) ** block_levels(seeds[7], (NB, R), ((0, 8),), -0.2, 0.2)), 0.05, 64.0),
        "block_ranks": with_ends(jax.random.randint(seeds[8], (NB,), R // 4, R + 1), jax.random.fold_in(seeds[8], 1), R // 4, R).astype(jnp.int32),
    }


highest = lax.Precision.HIGHEST
ridge_weight = 0.1

def kernel_tile(points, point_sq, center_block):
    center_sq = lax.optimization_barrier(jnp.sum(jnp.square(center_block.astype(jnp.float32)), axis=1))
    cross_term = lax.dot_general(points, center_block, (((1,), (1,)), ((), ())), preferred_element_type=jnp.float32)
    distance = point_sq[:, None] + center_sq[None, :] - 2.0 * cross_term
    return jnp.exp(-(1.0 / D) * distance).astype(jnp.bfloat16)

def solve_step(state, inputs):
    inv_block, left_block, right_block, decay_block, grad_block = inputs
    rhs_block = grad_block - jnp.dot(left_block, state, precision=highest)
    solved = jnp.dot(inv_block, rhs_block, precision=highest)
    state = decay_block[:, None] * state + jnp.dot(right_block.T, solved, precision=highest)
    return (state, solved)

def reference(points, centers, coeffs, targets, diag_inv, low_left, low_right, decay_rates, block_ranks):
    block_width = M // 16
    block_count = M // block_width
    point_sq = lax.optimization_barrier(jnp.sum(jnp.square(points.astype(jnp.float32)), axis=1))
    center_blocks = centers.reshape(block_count, block_width, D)
    coeff_blocks = coeffs.reshape(block_count, block_width, L)

    def add_block(running, paired):
        kernel_part = kernel_tile(points, point_sq, paired[0])
        return (running + jnp.dot(kernel_part, paired[1], preferred_element_type=jnp.float32), None)
    prediction, _ = lax.scan(add_block, jnp.zeros((N, L), jnp.float32), (center_blocks, coeff_blocks))
    residual = (jax.nn.sigmoid(prediction) - targets.astype(jnp.float32)).astype(jnp.bfloat16)

    def grad_piece(center_block):
        kernel_part = kernel_tile(points, point_sq, center_block)
        return lax.dot_general(kernel_part, residual, (((0,), (0,)), ((), ())), preferred_element_type=jnp.float32)
    summed = lax.map(grad_piece, center_blocks).reshape(M, L)
    gradient = summed * (1.0 / math.sqrt(N)) + ridge_weight * coeffs.astype(jnp.float32)
    rank_mask = (jnp.arange(R)[None, :] < block_ranks[:, None]).astype(jnp.float32)
    left_masked = low_left.astype(jnp.float32) * rank_mask[:, None, :]
    right_masked = low_right.astype(jnp.float32) * rank_mask[:, None, :]
    decays = jnp.exp(-decay_rates / NB)
    grad_blocks = gradient.reshape(NB, B, L)
    _, solved = lax.scan(solve_step, jnp.zeros((R, L), jnp.float32), (diag_inv, left_masked, right_masked, decays, grad_blocks))
    return solved.reshape(M, L)
```

```python
import functools
import math

import jax
import jax.numpy as jnp
from jax import lax
from jax.experimental import pallas as pl
from jax.experimental.pallas import tpu as pltpu
from jax.sharding import PartitionSpec as P

highest = lax.Precision.HIGHEST
high = lax.Precision.HIGH
ridge_weight = 0.1
decay_period = 128.0
lanes = 128


def split_three(x):
    a = lax.reduce_precision(x, 8, 7)
    b = lax.reduce_precision(x - a, 8, 7)
    c = x - a - b
    return [v.astype(jnp.bfloat16)[:, None] for v in (a, b, c)]


def left_form(rows):
    count, width = rows.shape
    norms = jnp.sum(jnp.square(rows.astype(jnp.float32)), axis=1) * (-1.0 / width)
    one = jnp.ones((count, 1), jnp.bfloat16)
    pad = jnp.zeros((count, lanes - width - 6), jnp.bfloat16)
    return jnp.concatenate(
        [rows * jnp.bfloat16(2.0 / width)] + split_three(norms) + [one, one, one, pad], axis=1
    )


def right_form(rows):
    count, width = rows.shape
    norms = jnp.sum(jnp.square(rows.astype(jnp.float32)), axis=1) * (-1.0 / width)
    one = jnp.ones((count, 1), jnp.bfloat16)
    pad = jnp.zeros((count, lanes - width - 6), jnp.bfloat16)
    return jnp.concatenate([rows, one, one, one] + split_three(norms) + [pad], axis=1)


def apply_body(tile, steps, a_ref, b_ref, v_ref, o_ref):
    total = None
    for j in range(steps):
        cols = slice(j * tile, (j + 1) * tile)
        logits = lax.dot_general(
            a_ref[...], b_ref[:, cols], (((1,), (0,)), ((), ())),
            preferred_element_type=jnp.float32,
        )
        part = jnp.dot(
            jnp.exp(logits).astype(jnp.bfloat16), v_ref[cols, :],
            preferred_element_type=jnp.float32,
        )
        total = part if total is None else total + part

    @pl.when(pl.program_id(1) == 0)
    def _():
        o_ref[...] = total

    @pl.when(pl.program_id(1) > 0)
    def _():
        o_ref[...] += total


def kernel_apply(a, b_t, v, tm=512, tk=1024, steps=2):
    m, n, labels = a.shape[0], b_t.shape[1], v.shape[1]
    tm = min(tm, m)
    tk = min(tk, n)
    while n % (tk * steps):
        steps -= 1
    span = tk * steps
    return pl.pallas_call(
        functools.partial(apply_body, tk, steps),
        out_shape=jax.ShapeDtypeStruct((m, labels), jnp.float32),
        grid=(m // tm, n // span),
        in_specs=[
            pl.BlockSpec((tm, lanes), lambda i, j: (i, 0)),
            pl.BlockSpec((lanes, span), lambda i, j: (0, j)),
            pl.BlockSpec((span, labels), lambda i, j: (j, 0)),
        ],
        out_specs=pl.BlockSpec((tm, labels), lambda i, j: (i, 0)),
        compiler_params=pltpu.CompilerParams(vmem_limit_bytes=40 * 1024 * 1024),
        cost_estimate=pl.CostEstimate(
            flops=2 * m * n * (lanes + labels) * 2,
            bytes_accessed=(m + n) * lanes * 2 + n * labels * 2 + m * labels * 4,
            transcendentals=m * n,
        ),
    )(a, b_t, v)


def body(points, centers, coeffs, targets, diag_inv, low_left, low_right, decay_rates, block_ranks):
    samp, ind = lax.axis_size("samp"), lax.axis_size("ind")
    samp_at, ind_at = lax.axis_index("samp"), lax.axis_index("ind")
    rows, width = points.shape
    inducing_rows, labels = coeffs.shape
    blocks, size, rank = low_left.shape
    chunks = 2
    chunk_rows = rows // chunks
    share = chunk_rows // ind
    own_count = inducing_rows // samp

    all_points = lax.all_gather(points, "samp", axis=0)
    point_left = left_form(points)
    center_right = right_form(centers).T

    residuals = []
    for c in range(chunks):
        part = kernel_apply(point_left[c * chunk_rows:(c + 1) * chunk_rows], center_right, coeffs)
        pred = lax.psum_scatter(part, "ind", scatter_dimension=0, tiled=True)
        own = lax.dynamic_slice_in_dim(targets, c * chunk_rows + ind_at * share, share, 0)
        resid = (jax.nn.sigmoid(pred) - own.astype(jnp.float32)).astype(jnp.bfloat16)
        residuals.append(lax.all_gather(resid, ("samp", "ind"), axis=0, tiled=True))

    own_centers = left_form(lax.dynamic_slice_in_dim(centers, samp_at * own_count, own_count, 0))
    point_right = [
        right_form(all_points[:, c * chunk_rows:(c + 1) * chunk_rows].reshape(-1, width)).T
        for c in range(chunks)
    ]

    mask = jnp.arange(rank)[None, :] < block_ranks[:, None]
    left = jnp.where(mask[:, None, :], low_left, 0).astype(jnp.float32)
    right = jnp.where(mask[:, None, :], low_right, 0).astype(jnp.float32)
    decays = jnp.exp(-decay_rates / decay_period)
    inv_left = jnp.einsum("kab,kbr->kar", diag_inv, left, precision=high)
    step_maps = decays[:, :, None] * jnp.eye(rank, dtype=jnp.float32) - jnp.einsum(
        "kar,kas->krs", right, inv_left, precision=high
    )
    eye = jnp.eye(rank, dtype=jnp.float32)
    current = jnp.pad(eye, ((0, 0), (0, blocks * rank)))
    maps = [current]
    for k in range(blocks):
        current = jnp.dot(step_maps[k], current, precision=high) + jnp.pad(
            eye, ((0, 0), ((k + 1) * rank, (blocks - 1 - k) * rank))
        )
        maps.append(current)
    state_maps = jnp.concatenate(maps[:-1], axis=0)
    exit_map = maps[-1][:, rank:]
    transfers = lax.all_gather(maps[-1][:, :rank], "ind", axis=0)
    entry = jnp.zeros((rank, ind * rank), jnp.float32)
    for d in range(ind - 1):
        moved = jnp.dot(transfers[d], entry, precision=high) + jnp.pad(
            eye, ((0, 0), (d * rank, (ind - 1 - d) * rank))
        )
        entry = jnp.where(d < ind_at, moved, entry)

    scaling = 1.0 / math.sqrt(rows * samp)
    first = kernel_apply(own_centers, point_right[0], residuals[0])
    half = own_count // 2
    gathered = []
    own_coeffs = lax.dynamic_slice_in_dim(coeffs, samp_at * own_count, own_count, 0)
    for h in range(2):
        rng = slice(h * half, (h + 1) * half)
        piece = first[rng] + kernel_apply(own_centers[rng], point_right[1], residuals[1])
        piece = piece * scaling + ridge_weight * own_coeffs[rng].astype(jnp.float32)
        gathered.append(lax.all_gather(piece, "samp", axis=0))
    gradient = jnp.concatenate(gathered, axis=1).reshape(blocks, size, labels)

    solved = jnp.einsum("kab,kbl->kal", diag_inv, gradient, precision=high)
    inputs = jnp.einsum("kar,kal->krl", right, solved, precision=high).reshape(blocks * rank, labels)
    offset = jnp.dot(exit_map, inputs, precision=high)
    offsets = lax.all_gather(offset, "ind", axis=0, tiled=True)
    local = jnp.dot(state_maps[:, rank:], inputs, precision=high)
    entering = jnp.dot(entry, offsets, precision=high)
    states = local + jnp.dot(state_maps[:, :rank], entering, precision=high)
    direction = solved - jnp.einsum(
        "kar,krl->kal", inv_left, states.reshape(blocks, rank, labels), precision=high
    )
    return direction.reshape(inducing_rows, labels)


def solution(mesh):
    return jax.shard_map(
        body,
        mesh=mesh,
        in_specs=(
            P("samp", None),
            P("ind", None),
            P("ind", None),
            P("samp", None),
            P("ind", None, None),
            P("ind", None, None),
            P("ind", None, None),
            P("ind", None),
            P("ind"),
        ),
        out_specs=P("ind", None),
        check_vma=False,
    )
```

```python
import functools
import math

import jax
import jax.numpy as jnp
from jax import lax
from jax.experimental import pallas as pl
from jax.experimental.pallas import tpu as pltpu
from jax.sharding import PartitionSpec as P

highest = lax.Precision.HIGHEST
high = lax.Precision.HIGH
ridge_weight = 0.1
decay_period = 128.0
lanes = 128


def split_three(x):
    a = lax.reduce_precision(x, 8, 7)
    b = lax.reduce_precision(x - a, 8, 7)
    c = x - a - b
    return [v.astype(jnp.bfloat16)[:, None] for v in (a, b, c)]


def left_form(rows):
    count, width = rows.shape
    turned = rows.T
    norms = jnp.sum(jnp.square(turned.astype(jnp.float32)), axis=0) * (-1.0 / width)
    pieces = [v.T for v in split_three(norms)]
    pad = jnp.zeros((lanes - width - 6, count), jnp.bfloat16)
    one = jnp.ones((3, count), jnp.bfloat16)
    return jnp.concatenate([turned * jnp.bfloat16(2.0 / width)] + pieces + [one, pad], axis=0).T


def right_form(rows):
    count, width = rows.shape
    turned = rows.T
    norms = jnp.sum(jnp.square(turned.astype(jnp.float32)), axis=0) * (-1.0 / width)
    pieces = [v.T for v in split_three(norms)]
    pad = jnp.zeros((lanes - width - 6, count), jnp.bfloat16)
    return jnp.concatenate([turned, jnp.ones((3, count), jnp.bfloat16)] + pieces + [pad], axis=0)


def halves(x):
    top = x.astype(jnp.bfloat16)
    return top, (x - top.astype(jnp.float32)).astype(jnp.bfloat16)


def solve_body(inv_ref, grad_ref, right_ref, solved_ref, input_ref):
    inv_top, inv_low = halves(inv_ref[0])
    grad_top, grad_low = halves(grad_ref[0])
    dot = functools.partial(jnp.dot, preferred_element_type=jnp.float32)
    solved = dot(inv_top, grad_low) + dot(inv_low, grad_top) + dot(inv_top, grad_top)
    solved_ref[0] = solved
    top, low = halves(solved)
    right = right_ref[0]
    input_ref[0] = dot(right, low) + dot(right, top)


def block_solve(inv, grad, right_t):
    blocks, size, labels = grad.shape
    rank = right_t.shape[1]
    spec = lambda *shape: pl.BlockSpec((1,) + shape, lambda k: (k, 0, 0))
    return pl.pallas_call(
        solve_body,
        out_shape=(
            jax.ShapeDtypeStruct((blocks, size, labels), jnp.float32),
            jax.ShapeDtypeStruct((blocks, rank, labels), jnp.float32),
        ),
        grid=(blocks,),
        in_specs=[spec(size, size), spec(size, labels), spec(rank, size)],
        out_specs=(spec(size, labels), spec(rank, labels)),
        compiler_params=pltpu.CompilerParams(vmem_limit_bytes=32 * 1024 * 1024),
        cost_estimate=pl.CostEstimate(
            flops=6 * blocks * size * labels * (size + rank),
            bytes_accessed=blocks * size * (size + 2 * labels) * 4,
            transcendentals=0,
        ),
    )(inv, grad, right_t)


def partner(at, step, count):
    return at ^ step if count & (count - 1) == 0 else (at + step) % count


def exchange(block, axis):
    count = lax.axis_size(axis)
    return [block] + [
        lax.ppermute(block, axis, [(partner(i, d, count), i) for i in range(count)])
        for d in range(1, count)
    ]


def apply_body(tile, steps, a_ref, b_ref, v_ref, o_ref):
    total = None
    for j in range(steps):
        cols = slice(j * tile, (j + 1) * tile)
        logits = lax.dot_general(
            a_ref[...], b_ref[:, cols], (((1,), (0,)), ((), ())),
            preferred_element_type=jnp.float32,
        )
        part = jnp.dot(
            jnp.exp(logits).astype(jnp.bfloat16), v_ref[cols, :],
            preferred_element_type=jnp.float32,
        )
        total = part if total is None else total + part

    @pl.when(pl.program_id(1) == 0)
    def _():
        o_ref[...] = total

    @pl.when(pl.program_id(1) > 0)
    def _():
        o_ref[...] += total


def kernel_apply(a, b_t, v, tm=512, tk=1024, steps=2):
    m, n, labels = a.shape[0], b_t.shape[1], v.shape[1]
    tm = min(tm, m)
    tk = min(tk, n)
    while n % (tk * steps):
        steps -= 1
    span = tk * steps
    return pl.pallas_call(
        functools.partial(apply_body, tk, steps),
        out_shape=jax.ShapeDtypeStruct((m, labels), jnp.float32),
        grid=(m // tm, n // span),
        in_specs=[
            pl.BlockSpec((tm, lanes), lambda i, j: (i, 0)),
            pl.BlockSpec((lanes, span), lambda i, j: (0, j)),
            pl.BlockSpec((span, labels), lambda i, j: (j, 0)),
        ],
        out_specs=pl.BlockSpec((tm, labels), lambda i, j: (i, 0)),
        compiler_params=pltpu.CompilerParams(vmem_limit_bytes=40 * 1024 * 1024),
        cost_estimate=pl.CostEstimate(
            flops=2 * m * n * (lanes + labels) * 2,
            bytes_accessed=(m + n) * lanes * 2 + n * labels * 2 + m * labels * 4,
            transcendentals=m * n,
        ),
    )(a, b_t, v)


def body(points, centers, coeffs, targets, diag_inv, low_left, low_right, decay_rates, block_ranks):
    samp, ind = lax.axis_size("samp"), lax.axis_size("ind")
    samp_at, ind_at = lax.axis_index("samp"), lax.axis_index("ind")
    rows, width = points.shape
    inducing_rows, labels = coeffs.shape
    blocks, size, rank = low_left.shape
    share = rows // ind
    own_count = inducing_rows // samp

    point_right = exchange(right_form(points), "samp")
    part = kernel_apply(left_form(points), right_form(centers), coeffs)
    pred = lax.psum_scatter(part, "ind", scatter_dimension=0, tiled=True)
    own_targets = lax.dynamic_slice_in_dim(targets, ind_at * share, share, 0)
    own_centers = left_form(lax.dynamic_slice_in_dim(centers, samp_at * own_count, own_count, 0))

    mask = jnp.arange(rank)[None, :] < block_ranks[:, None]
    left = jnp.where(mask[:, None, :], low_left, 0).astype(jnp.float32)
    right = jnp.where(mask[:, None, :], low_right, 0).astype(jnp.float32)
    decays = jnp.exp(-decay_rates / decay_period)
    inv_left = jnp.einsum("kab,kbr->kar", diag_inv, left, precision=high)
    step_maps = decays[:, :, None] * jnp.eye(rank, dtype=jnp.float32) - jnp.einsum(
        "kar,kas->krs", right, inv_left, precision=high
    )
    own_targets, step_maps = lax.optimization_barrier((own_targets, step_maps))

    resid = (jax.nn.sigmoid(pred) - own_targets.astype(jnp.float32)).astype(jnp.bfloat16)
    residual = lax.all_gather(resid, "ind", axis=0, tiled=True)
    summed = None
    for form, piece in zip(point_right, exchange(residual, "samp")):
        term = kernel_apply(own_centers, form, piece)
        summed = term if summed is None else summed + term
    scaling = 1.0 / math.sqrt(rows * samp)
    own_coeffs = lax.dynamic_slice_in_dim(coeffs, samp_at * own_count, own_count, 0)
    own_gradient = summed * scaling + ridge_weight * own_coeffs.astype(jnp.float32)

    own_gradient, step_maps = lax.optimization_barrier((own_gradient, step_maps))
    eye = jnp.eye(rank, dtype=jnp.float32)
    current = jnp.pad(eye, ((0, 0), (0, blocks * rank)))
    maps = [current]
    for k in range(blocks):
        current = jnp.dot(step_maps[k], current, precision=high) + jnp.pad(
            eye, ((0, 0), ((k + 1) * rank, (blocks - 1 - k) * rank))
        )
        maps.append(current)
    state_maps = jnp.concatenate(maps[:-1], axis=0)
    exit_map = maps[-1][:, rank:]
    transfers = lax.all_gather(maps[-1][:, :rank], "ind", axis=0)
    entry = jnp.zeros((rank, ind * rank), jnp.float32)
    for d in range(ind - 1):
        moved = jnp.dot(transfers[d], entry, precision=high) + jnp.pad(
            eye, ((0, 0), (d * rank, (ind - 1 - d) * rank))
        )
        entry = jnp.where(d < ind_at, moved, entry)

    gradient = jnp.zeros((inducing_rows, labels), jnp.float32)
    for d, piece in enumerate(exchange(own_gradient, "samp")):
        gradient = lax.dynamic_update_slice_in_dim(
            gradient, piece, partner(samp_at, d, samp) * own_count, 0
        )
    gradient = gradient.reshape(blocks, size, labels)

    right_t = jnp.swapaxes(jnp.where(mask[:, None, :], low_right, 0), 1, 2)
    solved, inputs = block_solve(diag_inv, gradient, right_t)
    inputs = inputs.reshape(blocks * rank, labels)
    offset = jnp.dot(exit_map, inputs, precision=high)
    offsets = lax.all_gather(offset, "ind", axis=0, tiled=True)
    local = jnp.dot(state_maps[:, rank:], inputs, precision=high)
    entering = jnp.dot(entry, offsets, precision=high)
    states = local + jnp.dot(state_maps[:, :rank], entering, precision=high)
    direction = solved - jnp.einsum(
        "kar,krl->kal", inv_left, states.reshape(blocks, rank, labels), precision=high
    )
    return direction.reshape(inducing_rows, labels)


def solution(mesh):
    return jax.shard_map(
        body,
        mesh=mesh,
        in_specs=(
            P("samp", None),
            P("ind", None),
            P("ind", None),
            P("samp", None),
            P("ind", None, None),
            P("ind", None, None),
            P("ind", None, None),
            P("ind", None),
            P("ind"),
        ),
        out_specs=P("ind", None),
        check_vma=False,
    )
```
